512 devices in a mesh: prow: 32 (over z, core), pcol: 16 (over y, x).
Axes of the slice: x: 4, y: 4, z: 16, core: 2. Of those that a mesh axis runs over, the one named last changes fastest.
Arguments:
- diag_block: float32 [256, 256], P('prow'), as said below
- panel: float32 [65536, 256], P(('prow', 'pcol')), may hold values from -4 to 4
- trailing: float32 [65536, 4096], P('prow', 'pcol'), may hold values from -6 to 6
Outputs:
- updated: float32 [65536, 4096], P('prow', 'pcol')
- solved: float32 [65536, 256], P(('prow', 'pcol'))
The draws below stay inside these ranges and needn't reach their ends.
Inputs may be any that keep to these rules, and one draw needn't show every extreme that they name: diag_block is symmetric positive definite.
All inputs are finite; a program needn't handle non-finite values.
Results may differ from the reference program's by a relative error of at most 0.00007.
Values sent between devices are 32-bit elements; how exact they have to be, the bound alone decides.
A program may use at most 64 MiB of HBM per device.

```python
import jax
import jax.numpy as jnp
from jax import lax

NB = 256
RB_DEV = 8
ROWS = 65536
COLS = 4096
N_PCOL = 16


def draw_diag_block(key, part):
    key = jax.random.fold_in(key, 11)
    first, second = jax.random.split(key)
    upper = jax.random.uniform(first, (NB, NB), jnp.float32, -1.0, 1.0)
    symmetric = (upper + upper.T) * (0.5 / NB)
    leading = 1.1 + jax.random.uniform(second, (NB,), jnp.float32, 0.0, 1.5)
    identity = jnp.eye(NB, dtype=jnp.float32)
    return symmetric * (1.0 - identity) + leading[:, None] * identity


def block_levels(key, extent, cuts, low, high):
    def one(axis_at, blocks):
        heights = jax.random.uniform(jax.random.fold_in(jax.random.fold_in(key, 6), axis_at), (blocks,), jnp.float32, low / len(cuts), high / len(cuts))
        return jnp.repeat(jnp.exp(heights), extent[axis_at] // blocks).reshape((-1,) + (1,) * (len(extent) - axis_at - 1))

    loudness = one(*cuts[0])
    for cut in cuts[1:]:
        loudness = loudness * one(*cut)
    return loudness


def normal_values(rng, extent, width, limit, pieces=(), held_as=jnp.bfloat16):
    level = block_levels(rng, extent, pieces, -0.22, 0.18) if pieces else 1.0
    values = jax.random.normal(rng, extent, jnp.float32) * width * level
    return jnp.minimum(jnp.maximum(values, -limit), limit).astype(held_as)


def setup_inputs(seed: int = 0) -> dict:
    key_of = jax.random.split(jax.random.key(seed), 4)
    return {
        "diag_block": draw_diag_block(jax.random.fold_in(key_of[3], 71), 0),
        "panel": normal_values(key_of[1], (ROWS, NB), 0.25, 4.0, ((0, 512),), jnp.float32),
        "trailing": normal_values(key_of[2], (ROWS, COLS), 1.0, 6.0, ((0, 32), (1, 16)), jnp.float32),
    }


def reference(diag_block, panel, trailing):
    factor = jnp.linalg.cholesky(diag_block)
    identity = jnp.eye(NB, dtype=jnp.float32)
    inverse = lax.linalg.triangular_solve(factor, identity, left_side=True, lower=True)
    solved = jnp.dot(panel.astype(jnp.float32), inverse.T.astype(jnp.float32), precision=lax.Precision.HIGHEST, preferred_element_type=jnp.float32)
    tiles = [solved[j * RB_DEV * NB:j * RB_DEV * NB + NB] for j in range(N_PCOL)]
    partner = jnp.concatenate(tiles, axis=0)
    product = lax.dot_general(solved.astype(jnp.float32), partner.astype(jnp.float32), (((1,), (1,)), ((), ())), precision=lax.Precision.HIGHEST, preferred_element_type=jnp.float32)
    updated = trailing - product
    return (updated, solved)
```

```python
import functools

import jax
import jax.numpy as jnp
from jax import lax
from jax.experimental import pallas as pl
from jax.experimental.pallas import tpu as pltpu
from jax.sharding import PartitionSpec as P

HI = lax.Precision.HIGHEST
F32 = jnp.float32
NBK = 16
H = 128

def sub(x, s):
    return jnp.broadcast_to(x[s:s + 1, :], (8, 128))

def lane(x, c):
    return jnp.broadcast_to(x[:, c:c + 1], (8, 128))

def dot_tn(a, b):
    return lax.dot_general(a, b, (((0,), (0,)), ((), ())), precision=HI, preferred_element_type=F32)

def dot_nn(a, b):
    return lax.dot_general(a, b, (((1,), (0,)), ((), ())), precision=HI, preferred_element_type=F32)

def dot_nt(a, b):
    return lax.dot_general(a, b, (((1,), (1,)), ((), ())), precision=HI, preferred_element_type=F32)


def stage(e_ref, r_ref, u_ref, y_ref, tiles, unroll=False):
    iota = lax.broadcasted_iota(jnp.int32, (8, 128), 0)

    def body(k, carry):
        u_prev = u_ref[...]
        e_ref[0:H, :] = e_ref[0:H, :] - dot_tn(u_prev[:, 0:H], u_prev)

        r = [[r_ref[8 * g:8 * g + 8, 128 * t:128 * t + 128] for t in range(tiles + 1)] for g in range(2)]
        b = [[lane(r[g][0], j) if (g == 1 or j < 8) else None for g in range(2)] for j in range(16)]
        rot = [pltpu.roll(r[g][0], H - NBK, 1) for g in range(2)]
        nxt = jnp.concatenate(rot, axis=0).T[0:16, :]
        gm = [[lane(nxt[8 * g:8 * g + 8, :], j) for g in range(2)] for j in range(16)]
        for g in range(2):
            r[g][0] = rot[g]
        scale = [None, None]
        rows = []
        gs = []
        for j in range(16):
            gj, sj = divmod(j, 8)
            p = sub(b[j][gj], sj)
            f = 1.0 / p
            rs = lax.rsqrt(p)
            m = [None, None]
            for g in range(gj, 2):
                m[g] = b[j][g] * f
            scale[gj] = rs if sj == 0 else jnp.where(iota >= sj, rs, scale[gj])
            g0 = gm[j][0] * f
            g1 = gm[j][1] * f
            gs.append((g0, g1))
            for c in range(j + 1, 16):
                gc, sc = divmod(c, 8)
                a = sub(b[j][gc], sc)
                for g in range(gc, 2):
                    b[c][g] = b[c][g] - m[g] * a
                gm[c][0] = gm[c][0] - g0 * a
                gm[c][1] = gm[c][1] - g1 * a
            row = [sub(r[gj][t], sj) for t in range(tiles + 1)]
            rows.append(row)
            for g in range(gj, 2):
                mm = jnp.where(iota > sj, m[g], 0.0) if g == gj else m[g]
                if g == gj and sj == 7:
                    continue
                for t in range(tiles + 1):
                    r[g][t] = r[g][t] - mm * row[t]
        base = pl.multiple_of((k + 1) * NBK, NBK)
        for g in range(2):
            for t in range(tiles + 1):
                acc = e_ref[pl.ds(base + 8 * g, 8), 128 * t:128 * t + 128]
                if t == 0:
                    acc = pltpu.roll(acc, lax.rem(2 * H - NBK * (k + 1), H), 1)
                for j in range(16):
                    acc = acc - gs[j][g] * rows[j][t]
                r_ref[8 * g:8 * g + 8, 128 * t:128 * t + 128] = acc
        here = pl.multiple_of(k * NBK, NBK)
        for g in range(2):
            for t in range(tiles + 1):
                v = r[g][t] * scale[g]
                if t == 0:
                    v = pltpu.roll(v, lax.rem(NBK * (k + 1), H), 1)
                else:
                    y_ref[pl.ds(here + 8 * g, 8), 128 * (t - 1):128 * t] = v
                u_ref[8 * g:8 * g + 8, 128 * t:128 * t + 128] = v
        return carry

    r_ref[...] = e_ref[0:16, :]
    u_ref[...] = jnp.zeros_like(u_ref)
    if unroll:
        for k in range(8):
            body(k, 0)
    else:
        lax.fori_loop(0, 8, body, 0)


def chol_inverse(a_ref, w_ref, e1, r1, u1, y1, e2, r2, u2, y2, unroll=False):
    eye = (lax.broadcasted_iota(jnp.int32, (H, H), 0) == lax.broadcasted_iota(jnp.int32, (H, H), 1)).astype(F32)
    e1[0:H, 0:2 * H] = a_ref[0:H, :]
    e1[0:H, 2 * H:3 * H] = eye
    e1[H:, :] = jnp.zeros_like(e1[H:, :])
    stage(e1, r1, u1, y1, 2, unroll)
    u12 = y1[:, 0:H]
    e2[0:H, 0:H] = a_ref[H:2 * H, H:2 * H] - dot_tn(u12, u12)
    e2[0:H, H:2 * H] = eye
    e2[H:, :] = jnp.zeros_like(e2[H:, :])
    v = dot_tn(u12, y1[:, H:2 * H])
    stage(e2, r2, u2, y2, 1, unroll)
    w_ref[0:H, 0:H] = y1[:, H:2 * H]
    w_ref[0:H, H:2 * H] = jnp.zeros((H, H), F32)
    w_ref[H:2 * H, 0:H] = -dot_nn(y2[...], v)
    w_ref[H:2 * H, H:2 * H] = y2[...]


SCRATCH = [pltpu.VMEM((144, 384), F32), pltpu.VMEM((16, 384), F32), pltpu.VMEM((16, 384), F32), pltpu.VMEM((128, 256), F32),
           pltpu.VMEM((144, 256), F32), pltpu.VMEM((16, 256), F32), pltpu.VMEM((16, 256), F32), pltpu.VMEM((128, 128), F32)]


MESH = pl.DeviceIdType.MESH
BF16 = jnp.bfloat16


def remote(src, dst, send, recv, to):
    return pltpu.make_async_remote_copy(
        src_ref=src, dst_ref=dst, send_sem=send, recv_sem=recv, device_id=to, device_id_type=MESH
    )


def gather_and_factor(
    diag_ref, panel_ref, pa_ref, pb_ref, q_ref, w_ref,
    d_ref, a_ref, e1, r1, u1, y1, e2, r2, u2, y2,
    d1_send, d1_recv, d2_send, d2_recv, q1_send, q1_recv, q2_send, q2_recv, q3_send, q3_recv,
    xa_send, xa_recv, yb_send, yb_recv, ya_send, ya_recv, xb_send, xb_recv, own_sem,
):
    prow, pcol = lax.axis_index("prow"), lax.axis_index("pcol")
    z, core = prow // 2, prow % 2
    y, x = pcol // 4, pcol % 4
    peer = (z * 2 + 1 - core, pcol)
    source = jnp.logical_and(prow < 16, pcol < 2)
    self_lead = jnp.logical_and(source, prow == pcol)

    def along_z(d):
        return (lax.rem(z + d, 16) * 2 + core, pcol)

    def along_x(d):
        return (prow, y * 4 + lax.rem(x + d, 4))

    def along_y(d):
        return (prow, lax.rem(y + d, 4) * 4 + x)

    barrier = pltpu.get_barrier_semaphore()

    def greet(to):
        pl.semaphore_signal(barrier, inc=1, device_id=to, device_id_type=MESH)

    def greet_z(d, carry):
        greet(along_z(d))
        return carry

    greet(peer)
    for d in (1, 2, 3):
        greet(along_x(d))
        greet(along_y(d))

    @pl.when(jnp.logical_not(self_lead))
    def _():
        greet((pcol, core))

    lax.fori_loop(1, 16, greet_z, 0)
    extra = jnp.where(source, 16, 0) - jnp.where(self_lead, 1, 0)
    pl.semaphore_wait(barrier, 22 + extra)

    def d1(d):
        return remote(diag_ref, d_ref.at[core, z], d1_send.at[d], d1_recv.at[d], along_z(d))

    def start_d1(d, carry):
        d1(d).start()
        return carry

    lax.fori_loop(1, 16, start_d1, 0)

    def q1(t):
        rows = panel_ref.at[pl.ds(pl.multiple_of(t * 8, 8), 8), :]
        return remote(rows, q_ref.at[pcol, t], q1_send.at[t], q1_recv.at[0], (t * 2 + pcol, prow))

    own_lead = pltpu.make_async_copy(panel_ref.at[pl.ds(0, 8), :], q_ref.at[core, z], own_sem.at[2])

    @pl.when(source)
    def _():
        def start_q1(t, carry):
            @pl.when(jnp.logical_not(jnp.logical_and(self_lead, t == 0)))
            def _():
                q1(t).start()
            return carry

        lax.fori_loop(0, 16, start_q1, 0)

    @pl.when(self_lead)
    def _():
        own_lead.start()

    top, low = panel_ref.at[pl.ds(0, 64), :], panel_ref.at[pl.ds(64, 64), :]

    def xa(d):
        return remote(top, pa_ref.at[y, x], xa_send.at[d], xa_recv.at[d], along_x(d))

    def yb(d):
        return remote(low, pb_ref.at[y, x], yb_send.at[d], yb_recv.at[d], along_y(d))

    own_top = pltpu.make_async_copy(top, pa_ref.at[y, x], own_sem.at[0])
    own_low = pltpu.make_async_copy(low, pb_ref.at[y, x], own_sem.at[1])
    for d in (1, 3, 2):
        xa(d).start()
        yb(d).start()
    own_top.start()
    own_low.start()
    d_ref[core, z] = diag_ref[...]

    def wait_d1(d, carry):
        d1(d).wait()
        return carry

    lax.fori_loop(1, 16, wait_d1, 0)
    d2 = remote(d_ref.at[core], d_ref.at[core], d2_send.at[0], d2_recv.at[0], peer)
    d2.start()

    @pl.when(jnp.logical_not(self_lead))
    def _():
        remote(q_ref.at[core, z], q_ref.at[core, z], q1_send.at[0], q1_recv.at[0], peer).wait_recv()

    @pl.when(self_lead)
    def _():
        own_lead.wait()

    def q2(d):
        return remote(q_ref.at[core, z], q_ref.at[core, z], q2_send.at[d], q2_recv.at[d], along_z(d))

    def start_q2(d, carry):
        q2(d).start()
        return carry

    lax.fori_loop(1, 16, start_q2, 0)

    own_top.wait()
    own_low.wait()
    for d in (1, 3, 2):
        xa(d).wait()
        yb(d).wait()

    def ya(d):
        return remote(pa_ref.at[y], pa_ref.at[y], ya_send.at[d], ya_recv.at[d], along_y(d))

    def xb(d):
        return remote(pb_ref.at[:, x], pb_ref.at[:, x], xb_send.at[d], xb_recv.at[d], along_x(d))

    for d in (1, 3, 2):
        ya(d).start()
        xb(d).start()

    d2.wait()
    for t in range(16):
        for c in range(2):
            a_ref[t * 16 + c * 8:t * 16 + c * 8 + 8, :] = d_ref[c, t]

    chol_inverse(a_ref, w_ref, e1, r1, u1, y1, e2, r2, u2, y2)

    def wait_q2(d, carry):
        q2(d).wait()
        return carry

    lax.fori_loop(1, 16, wait_q2, 0)
    q3 = remote(q_ref.at[core], q_ref.at[core], q3_send.at[0], q3_recv.at[0], peer)
    q3.start()

    @pl.when(source)
    def _():
        def wait_q1(t, carry):
            @pl.when(jnp.logical_not(jnp.logical_and(self_lead, t == 0)))
            def _():
                q1(t).wait_send()
            return carry

        lax.fori_loop(0, 16, wait_q1, 0)

    for d in (1, 3, 2):
        ya(d).wait()
        xb(d).wait()
    q3.wait()


def halves(v):
    high = v.astype(BF16)
    return high, (v - high.astype(F32)).astype(BF16)


def dot3(a, b):
    def one(p, q):
        return lax.dot_general(p, q, (((1,), (1,)), ((), ())), preferred_element_type=F32)

    return one(a[0], b[0]) + (one(a[0], b[1]) + one(a[1], b[0]))


def update(pa_ref, pb_ref, t_ref, w_ref, q_ref, own_ref, u_ref, s_ref, wh, wl, qh, ql):
    @pl.when(pl.program_id(0) == 0)
    def _():
        w = halves(w_ref[...])
        wh[...], wl[...] = w
        qh[...], ql[...] = halves(dot3(halves(q_ref[...]), w))
        s_ref[...] = dot3(halves(own_ref[...]), w)

    rows = jnp.concatenate([pa_ref[0], pb_ref[0], pa_ref[1], pb_ref[1]], axis=0)
    solved = dot3(halves(rows), (wh[...], wl[...]))
    u_ref[...] = t_ref[...] - dot3(halves(solved), (qh[...], ql[...]))


def per_device(diag_block, panel, trailing):
    hbm = pl.BlockSpec(memory_space=pl.ANY)
    vmem = pl.BlockSpec(memory_space=pltpu.VMEM)
    dma = pltpu.SemaphoreType.DMA
    pa, pb, q, w = pl.pallas_call(
        gather_and_factor,
        out_shape=(
            jax.ShapeDtypeStruct((4, 4, 64, 256), F32),
            jax.ShapeDtypeStruct((4, 4, 64, 256), F32),
            jax.ShapeDtypeStruct((2, 16, 8, 256), F32),
            jax.ShapeDtypeStruct((256, 256), F32),
        ),
        in_specs=[vmem, hbm],
        out_specs=(hbm, hbm, hbm, vmem),
        scratch_shapes=[pltpu.VMEM((2, 16, 8, 256), F32), pltpu.VMEM((256, 256), F32)] + SCRATCH + [
            dma((16,)), dma((16,)), dma((1,)), dma((1,)), dma((16,)), dma((1,)), dma((16,)), dma((16,)), dma((1,)), dma((1,)),
            dma((4,)), dma((4,)), dma((4,)), dma((4,)), dma((4,)), dma((4,)), dma((4,)), dma((4,)), dma((3,)),
        ],
        compiler_params=pltpu.CompilerParams(collective_id=0, has_side_effects=True, vmem_limit_bytes=32 << 20),
    )(diag_block, panel)
    pa, pb, q = pa.reshape(16, 64, 256), pb.reshape(16, 64, 256), q.reshape(256, 256)

    def whole(rows):
        return pl.BlockSpec((rows, 256), lambda i: (0, 0))

    return pl.pallas_call(
        update,
        grid=(8,),
        out_shape=(jax.ShapeDtypeStruct((2048, 256), F32), jax.ShapeDtypeStruct((128, 256), F32)),
        in_specs=[
            pl.BlockSpec((2, 64, 256), lambda i: (i, 0, 0)),
            pl.BlockSpec((2, 64, 256), lambda i: (i, 0, 0)),
            pl.BlockSpec((256, 256), lambda i: (i, 0)),
            whole(256), whole(256), whole(128),
        ],
        out_specs=(pl.BlockSpec((256, 256), lambda i: (i, 0)), whole(128)),
        scratch_shapes=[pltpu.VMEM((256, 256), BF16)] * 4,
        compiler_params=pltpu.CompilerParams(vmem_limit_bytes=32 << 20),
    )(pa, pb, trailing, w, q, panel)


def solution(mesh):
    in_specs = (P("prow", None), P(("prow", "pcol"), None), P("prow", "pcol"))
    out_specs = (P("prow", "pcol"), P(("prow", "pcol"), None))
    return jax.shard_map(
        per_device, mesh=mesh, in_specs=in_specs, out_specs=out_specs, check_vma=False
    )
```

```python
import functools

import jax
import jax.numpy as jnp
from jax import lax
from jax.experimental import pallas as pl
from jax.experimental.pallas import tpu as pltpu
from jax.sharding import PartitionSpec as P

HI = lax.Precision.HIGHEST
F32 = jnp.float32
NBK = 16
H = 128

def sub(x, s):
    return jnp.broadcast_to(x[s:s + 1, :], (8, 128))

def lane(x, c):
    return jnp.broadcast_to(x[:, c:c + 1], (8, 128))

def dot_tn(a, b):
    return lax.dot_general(a, b, (((0,), (0,)), ((), ())), precision=HI, preferred_element_type=F32)

def dot_nn(a, b):
    return lax.dot_general(a, b, (((1,), (0,)), ((), ())), precision=HI, preferred_element_type=F32)

def dot_nt(a, b):
    return lax.dot_general(a, b, (((1,), (1,)), ((), ())), precision=HI, preferred_element_type=F32)


def update_tn(u):
    rest = u
    parts = []
    for _ in range(3):
        parts.append(rest.astype(jnp.bfloat16))
        rest = rest - parts[-1].astype(F32)
    h, m, l = parts
    left = jnp.concatenate([p[:, 0:H] for p in (h, h, h, m, m, l)], axis=0)
    right = jnp.concatenate([h, m, l, h, m, h], axis=0)
    return lax.dot_general(left, right, (((0,), (0,)), ((), ())), preferred_element_type=F32)


def stage(e_ref, r_ref, u_ref, y_ref, tiles, unroll=False):
    iota = lax.broadcasted_iota(jnp.int32, (8, 128), 0)

    def body(k, carry):
        e_ref[0:H, :] = e_ref[0:H, :] - update_tn(u_ref[...])

        r = [[r_ref[8 * g:8 * g + 8, 128 * t:128 * t + 128] for t in range(tiles + 1)] for g in range(2)]
        b = [[lane(r[g][0], j) if (g == 1 or j < 8) else None for g in range(2)] for j in range(16)]
        rot = [pltpu.roll(r[g][0], H - NBK, 1) for g in range(2)]
        nxt = jnp.concatenate(rot, axis=0).T[0:16, :]
        gm = [[lane(nxt[8 * g:8 * g + 8, :], j) for g in range(2)] for j in range(16)]
        for g in range(2):
            r[g][0] = rot[g]
        scale = [None, None]
        rows = []
        gs = []
        for j in range(16):
            gj, sj = divmod(j, 8)
            if j == 0:
                p = sub(b[0][0], 0)
            f = 1.0 / p
            rs = lax.rsqrt(p)
            m = [None, None]
            for g in range(gj, 2):
                m[g] = b[j][g] * f
            scale[gj] = rs if sj == 0 else jnp.where(iota >= sj, rs, scale[gj])
            if j < 15:
                gn, sn = divmod(j + 1, 8)
                across = sub(b[j][gn], sn)
                p = sub(b[j + 1][gn], sn) - (across * across) * f
            g0 = gm[j][0] * f
            g1 = gm[j][1] * f
            gs.append((g0, g1))
            for c in range(j + 1, 16):
                gc, sc = divmod(c, 8)
                a = sub(b[j][gc], sc)
                for g in range(gc, 2):
                    b[c][g] = b[c][g] - m[g] * a
                gm[c][0] = gm[c][0] - g0 * a
                gm[c][1] = gm[c][1] - g1 * a
            row = [sub(r[gj][t], sj) for t in range(tiles + 1)]
            rows.append(row)
            for g in range(gj, 2):
                mm = jnp.where(iota > sj, m[g], 0.0) if g == gj else m[g]
                if g == gj and sj == 7:
                    continue
                for t in range(tiles + 1):
                    r[g][t] = r[g][t] - mm * row[t]
        base = pl.multiple_of((k + 1) * NBK, NBK)
        for g in range(2):
            for t in range(tiles + 1):
                acc = e_ref[pl.ds(base + 8 * g, 8), 128 * t:128 * t + 128]
                if t == 0:
                    acc = pltpu.roll(acc, lax.rem(2 * H - NBK * (k + 1), H), 1)
                for j in range(16):
                    acc = acc - gs[j][g] * rows[j][t]
                r_ref[8 * g:8 * g + 8, 128 * t:128 * t + 128] = acc
        here = pl.multiple_of(k * NBK, NBK)
        for g in range(2):
            for t in range(tiles + 1):
                v = r[g][t] * scale[g]
                if t == 0:
                    v = pltpu.roll(v, lax.rem(NBK * (k + 1), H), 1)
                else:
                    y_ref[pl.ds(here + 8 * g, 8), 128 * (t - 1):128 * t] = v
                u_ref[8 * g:8 * g + 8, 128 * t:128 * t + 128] = v
        return carry

    r_ref[...] = e_ref[0:16, :]
    u_ref[...] = jnp.zeros_like(u_ref)
    if unroll:
        for k in range(8):
            body(k, 0)
    else:
        lax.fori_loop(0, 8, body, 0)


def chol_inverse(a_ref, w_ref, e1, r1, u1, y1, e2, r2, u2, y2, unroll=False):
    eye = (lax.broadcasted_iota(jnp.int32, (H, H), 0) == lax.broadcasted_iota(jnp.int32, (H, H), 1)).astype(F32)
    e1[0:H, 0:2 * H] = a_ref[0:H, :]
    e1[0:H, 2 * H:3 * H] = eye
    e1[H:, :] = jnp.zeros_like(e1[H:, :])
    stage(e1, r1, u1, y1, 2, unroll)
    u12 = y1[:, 0:H]
    e2[0:H, 0:H] = a_ref[H:2 * H, H:2 * H] - dot_tn(u12, u12)
    e2[0:H, H:2 * H] = eye
    e2[H:, :] = jnp.zeros_like(e2[H:, :])
    v = dot_tn(u12, y1[:, H:2 * H])
    stage(e2, r2, u2, y2, 1, unroll)
    w_ref[0:H, 0:H] = y1[:, H:2 * H]
    w_ref[0:H, H:2 * H] = jnp.zeros((H, H), F32)
    w_ref[H:2 * H, 0:H] = -dot_nn(y2[...], v)
    w_ref[H:2 * H, H:2 * H] = y2[...]


SCRATCH = [pltpu.VMEM((144, 384), F32), pltpu.VMEM((16, 384), F32), pltpu.VMEM((16, 384), F32), pltpu.VMEM((128, 256), F32),
           pltpu.VMEM((144, 256), F32), pltpu.VMEM((16, 256), F32), pltpu.VMEM((16, 256), F32), pltpu.VMEM((128, 128), F32)]


MESH = pl.DeviceIdType.MESH
BF16 = jnp.bfloat16


def remote(src, dst, send, recv, to):
    return pltpu.make_async_remote_copy(
        src_ref=src, dst_ref=dst, send_sem=send, recv_sem=recv, device_id=to, device_id_type=MESH
    )


def each_along_z(act):
    act(8)

    def pair(k, carry):
        act(8 - k)
        act(8 + k)
        return carry

    lax.fori_loop(1, 8, pair, 0)


def gather_and_factor(
    diag_ref, panel_ref, pa_ref, pb_ref, q_ref, w_ref,
    own_ref, d_ref, a_ref, e1, r1, u1, y1, e2, r2, u2, y2,
    d1_send, d1_recv, dy_send, dy_recv, d2_send, d2_recv, q1_send, q1_recv, q2_send, q2_recv, q3_send, q3_recv,
    xa_send, xa_recv, yb_send, yb_recv, ya_send, ya_recv, xb_send, xb_recv, own_sem,
):
    prow, pcol = lax.axis_index("prow"), lax.axis_index("pcol")
    z, core = prow // 2, prow % 2
    y, x = pcol // 4, pcol % 4
    peer = (z * 2 + 1 - core, pcol)
    source = jnp.logical_and(prow < 16, pcol < 2)
    self_lead = jnp.logical_and(source, prow == pcol)

    def along_z(d):
        return (lax.rem(z + d, 16) * 2 + core, pcol)

    def along_x(d):
        return (prow, y * 4 + lax.rem(x + d, 4))

    def along_y(d):
        return (prow, lax.rem(y + d, 4) * 4 + x)

    barrier = pltpu.get_barrier_semaphore()

    def greet(to):
        pl.semaphore_signal(barrier, inc=1, device_id=to, device_id_type=MESH)

    each_along_z(lambda d: greet(along_z(d)))

    @pl.when(jnp.logical_not(self_lead))
    def _():
        greet((pcol, core))

    for d in (1, 2, 3):
        greet(along_x(d))
        greet(along_y(d))
    greet(peer)

    own = [
        pltpu.make_async_copy(panel_ref, own_ref, own_sem.at[0]),
        pltpu.make_async_copy(panel_ref.at[pl.ds(0, 64), :], pa_ref.at[y, x], own_sem.at[2]),
        pltpu.make_async_copy(panel_ref.at[pl.ds(64, 64), :], pb_ref.at[y, x], own_sem.at[3]),
    ]
    own_diag = pltpu.make_async_copy(diag_ref, d_ref.at[core, z % 4, z // 4], own_sem.at[1])
    own_lead = pltpu.make_async_copy(panel_ref.at[pl.ds(0, 8), :], q_ref.at[core, z], own_sem.at[4])
    mine = z % 4 == y
    for copy in own:
        copy.start()

    @pl.when(mine)
    def _():
        own_diag.start()
        own_diag.wait()

    @pl.when(self_lead)
    def _():
        own_lead.start()

    for copy in own:
        copy.wait()
    extra = jnp.where(source, 16, 0) - jnp.where(self_lead, 1, 0)
    pl.semaphore_wait(barrier, 22 + extra)

    def q1(d):
        t = lax.rem(z + d, 16)
        rows = own_ref.at[pl.ds(pl.multiple_of(t * 8, 8), 8), :]
        return remote(rows, q_ref.at[pcol, t], q1_send.at[d], q1_recv.at[0], (t * 2 + pcol, prow))

    def each_lead(act):
        @pl.when(source)
        def _():
            each_along_z(lambda d: act(q1(d)))

            @pl.when(jnp.logical_not(self_lead))
            def _():
                act(q1(0))

    each_lead(lambda copy: copy.start())

    def d1(d):
        rows = d_ref.at[core, z % 4, z // 4]
        return remote(rows, rows, d1_send.at[d], d1_recv.at[d], along_z(d))

    def each_d1(act):
        @pl.when(mine)
        def _():
            each_along_z(lambda d: act(d1(d)))

    each_d1(lambda copy: copy.start())

    def xa(d):
        return remote(pa_ref.at[y, x], pa_ref.at[y, x], xa_send.at[d], xa_recv.at[d], along_x(d))

    def yb(d):
        return remote(pb_ref.at[y, x], pb_ref.at[y, x], yb_send.at[d], yb_recv.at[d], along_y(d))

    for d in (2, 1, 3):
        xa(d).start()
        yb(d).start()

    for d in (1, 3, 2):
        xa(d).wait_recv()
        yb(d).wait_recv()

    def ya(d):
        return remote(pa_ref.at[y], pa_ref.at[y], ya_send.at[d], ya_recv.at[d], along_y(d))

    def xb(d):
        return remote(pb_ref.at[:, x], pb_ref.at[:, x], xb_send.at[d], xb_recv.at[d], along_x(d))

    for a in range(4):
        away = lax.rem(z - (4 * a + y) + 16, 16)

        @pl.when(away != 0)
        def _():
            d1(away).wait_recv()

    def dy(d):
        return remote(d_ref.at[core, y], d_ref.at[core, y], dy_send.at[d], dy_recv.at[d], along_y(d))

    for d in (2, 1, 3):
        dy(d).start()
    @pl.when(jnp.logical_not(self_lead))
    def _():
        remote(q_ref.at[core, z], q_ref.at[core, z], q1_send.at[0], q1_recv.at[0], peer).wait_recv()

    @pl.when(self_lead)
    def _():
        own_lead.wait()

    def q2(d):
        return remote(q_ref.at[core, z], q_ref.at[core, z], q2_send.at[d], q2_recv.at[d], along_z(d))

    each_along_z(lambda d: q2(d).start())

    for d in (2, 1, 3):
        ya(d).start()
        xb(d).start()
    for d in (1, 3, 2):
        dy(d).wait_recv()
    d2 = remote(d_ref.at[core], d_ref.at[core], d2_send.at[0], d2_recv.at[0], peer)
    d2.start()

    d2.wait_recv()
    for t in range(16):
        for c in range(2):
            a_ref[t * 16 + c * 8:t * 16 + c * 8 + 8, :] = d_ref[c, t % 4, t // 4]

    chol_inverse(a_ref, w_ref, e1, r1, u1, y1, e2, r2, u2, y2)

    each_along_z(lambda d: q2(d).wait_recv())
    q3 = remote(q_ref.at[core], q_ref.at[core], q3_send.at[0], q3_recv.at[0], peer)
    q3.start()
    for d in (1, 3, 2):
        ya(d).wait_recv()
        xb(d).wait_recv()
        xa(d).wait_send()
        yb(d).wait_send()
        ya(d).wait_send()
        xb(d).wait_send()
    each_d1(lambda copy: copy.wait_send())
    for d in (1, 2, 3):
        dy(d).wait_send()
    each_along_z(lambda d: q2(d).wait_send())
    each_lead(lambda copy: copy.wait_send())
    d2.wait_send()
    q3.wait()


def halves(v):
    high = v.astype(BF16)
    return high, (v - high.astype(F32)).astype(BF16)


def dot3(a, b):
    def one(p, q):
        return lax.dot_general(p, q, (((1,), (1,)), ((), ())), preferred_element_type=F32)

    return one(a[0], b[0]) + (one(a[0], b[1]) + one(a[1], b[0]))


def update(pa_ref, pb_ref, t_ref, w_ref, q_ref, own_ref, u_ref, s_ref, u_buf, s_buf, u_sem, s_sem):
    w = halves(w_ref[...])
    s_buf[...] = dot3(halves(own_ref[...]), w)
    s_copy = pltpu.make_async_copy(s_buf, s_ref, s_sem.at[0])
    s_copy.start()
    q = halves(dot3(halves(q_ref[...]), w))
    copies = []
    for i in range(8):
        rows = jnp.concatenate([pa_ref[2 * i], pb_ref[2 * i], pa_ref[2 * i + 1], pb_ref[2 * i + 1]], axis=0)
        solved = dot3(halves(rows), w)
        part = pl.ds(256 * i, 256)
        u_buf[part, :] = t_ref[part, :] - dot3(halves(solved), q)
        copy = pltpu.make_async_copy(u_buf.at[part, :], u_ref.at[part, :], u_sem.at[i])
        copy.start()
        copies.append(copy)
    for copy in copies:
        copy.wait()
    s_copy.wait()


def per_device(diag_block, panel, trailing):
    hbm = pl.BlockSpec(memory_space=pltpu.HBM)
    vmem = pl.BlockSpec(memory_space=pltpu.VMEM)
    dma = pltpu.SemaphoreType.DMA
    pa, pb, q, w = pl.pallas_call(
        gather_and_factor,
        out_shape=(
            jax.ShapeDtypeStruct((4, 4, 64, 256), F32),
            jax.ShapeDtypeStruct((4, 4, 64, 256), F32),
            jax.ShapeDtypeStruct((2, 16, 8, 256), F32),
            jax.ShapeDtypeStruct((256, 256), F32),
        ),
        in_specs=[hbm, hbm],
        out_specs=(vmem,) * 4,
        scratch_shapes=[pltpu.VMEM((128, 256), F32), pltpu.VMEM((2, 4, 4, 8, 256), F32), pltpu.VMEM((256, 256), F32)] + SCRATCH + [
            dma((16,)), dma((16,)), dma((4,)), dma((4,)), dma((1,)), dma((1,)), dma((16,)), dma((1,)), dma((16,)), dma((16,)), dma((1,)), dma((1,)),
            dma((4,)), dma((4,)), dma((4,)), dma((4,)), dma((4,)), dma((4,)), dma((4,)), dma((4,)), dma((5,)),
        ],
        cost_estimate=pl.CostEstimate(flops=10**10, bytes_accessed=80 * 10**6, transcendentals=0),
        compiler_params=pltpu.CompilerParams(collective_id=0, has_side_effects=True, vmem_limit_bytes=32 << 20),
    )(diag_block, panel)
    pa, pb, q = pa.reshape(16, 64, 256), pb.reshape(16, 64, 256), q.reshape(256, 256)
    return pl.pallas_call(
        update,
        out_shape=(jax.ShapeDtypeStruct((2048, 256), F32), jax.ShapeDtypeStruct((128, 256), F32)),
        in_specs=[vmem] * 6,
        out_specs=(hbm, hbm),
        scratch_shapes=[pltpu.VMEM((2048, 256), F32), pltpu.VMEM((128, 256), F32), dma((8,)), dma((1,))],
        compiler_params=pltpu.CompilerParams(vmem_limit_bytes=32 << 20),
    )(pa, pb, trailing, w, q, panel)


def solution(mesh):
    in_specs = (P("prow", None), P(("prow", "pcol"), None), P("prow", "pcol"))
    out_specs = (P("prow", "pcol"), P(("prow", "pcol"), None))
    return jax.shard_map(
        per_device, mesh=mesh, in_specs=in_specs, out_specs=out_specs, check_vma=False
    )
```

```python
import functools

import jax
import jax.numpy as jnp
from jax import lax
from jax.experimental import pallas as pl
from jax.experimental.pallas import tpu as pltpu
from jax.sharding import PartitionSpec as P

HI = lax.Precision.HIGHEST
F32 = jnp.float32
NBK = 16
H = 128

def sub(x, s):
    return jnp.broadcast_to(x[s:s + 1, :], (8, 128))

def lane(x, c):
    return jnp.broadcast_to(x[:, c:c + 1], (8, 128))

def dot_tn(a, b):
    return lax.dot_general(a, b, (((0,), (0,)), ((), ())), precision=HI, preferred_element_type=F32)

def dot_nn(a, b):
    return lax.dot_general(a, b, (((1,), (0,)), ((), ())), precision=HI, preferred_element_type=F32)

def dot_nt(a, b):
    return lax.dot_general(a, b, (((1,), (1,)), ((), ())), precision=HI, preferred_element_type=F32)


def update_tn(u):
    rest = u
    parts = []
    for _ in range(3):
        parts.append(rest.astype(jnp.bfloat16))
        rest = rest - parts[-1].astype(F32)
    h, m, l = parts
    left = jnp.concatenate([p[:, 0:H] for p in (h, h, h, m, m, l)], axis=0)
    right = jnp.concatenate([h, m, l, h, m, h], axis=0)
    return lax.dot_general(left, right, (((0,), (0,)), ((), ())), preferred_element_type=F32)


def stage(e_ref, r_ref, u_ref, y_ref, tiles, unroll=False):
    iota = lax.broadcasted_iota(jnp.int32, (8, 128), 0)

    def body(k, carry):
        e_ref[0:H, :] = e_ref[0:H, :] - update_tn(u_ref[...])

        r = [[r_ref[8 * g:8 * g + 8, 128 * t:128 * t + 128] for t in range(tiles + 1)] for g in range(2)]
        b = [[lane(r[g][0], j) if (g == 1 or j < 8) else None for g in range(2)] for j in range(16)]
        rot = [pltpu.roll(r[g][0], H - NBK, 1) for g in range(2)]
        nxt = jnp.concatenate(rot, axis=0).T[0:16, :]
        gm = [[lane(nxt[8 * g:8 * g + 8, :], j) for g in range(2)] for j in range(16)]
        for g in range(2):
            r[g][0] = rot[g]
        scale = [None, None]
        rows = []
        gs = []
        for j in range(16):
            gj, sj = divmod(j, 8)
            if j == 0:
                p = sub(b[0][0], 0)
            f = 1.0 / p
            rs = lax.rsqrt(p)
            m = [None, None]
            for g in range(gj, 2):
                m[g] = b[j][g] * f
            scale[gj] = rs if sj == 0 else jnp.where(iota >= sj, rs, scale[gj])
            if j < 15:
                gn, sn = divmod(j + 1, 8)
                across = sub(b[j][gn], sn)
                p = sub(b[j + 1][gn], sn) - (across * across) * f
            g0 = gm[j][0] * f
            g1 = gm[j][1] * f
            gs.append((g0, g1))
            for c in range(j + 1, 16):
                gc, sc = divmod(c, 8)
                a = sub(b[j][gc], sc)
                for g in range(gc, 2):
                    b[c][g] = b[c][g] - m[g] * a
                gm[c][0] = gm[c][0] - g0 * a
                gm[c][1] = gm[c][1] - g1 * a
            row = [sub(r[gj][t], sj) for t in range(tiles + 1)]
            rows.append(row)
            for g in range(gj, 2):
                mm = jnp.where(iota > sj, m[g], 0.0) if g == gj else m[g]
                if g == gj and sj == 7:
                    continue
                for t in range(tiles + 1):
                    r[g][t] = r[g][t] - mm * row[t]
        base = pl.multiple_of((k + 1) * NBK, NBK)
        for g in range(2):
            for t in range(tiles + 1):
                acc = e_ref[pl.ds(base + 8 * g, 8), 128 * t:128 * t + 128]
                if t == 0:
                    acc = pltpu.roll(acc, lax.rem(2 * H - NBK * (k + 1), H), 1)
                for j in range(16):
                    acc = acc - gs[j][g] * rows[j][t]
                r_ref[8 * g:8 * g + 8, 128 * t:128 * t + 128] = acc
        here = pl.multiple_of(k * NBK, NBK)
        for g in range(2):
            for t in range(tiles + 1):
                v = r[g][t] * scale[g]
                if t == 0:
                    v = pltpu.roll(v, lax.rem(NBK * (k + 1), H), 1)
                else:
                    y_ref[pl.ds(here + 8 * g, 8), 128 * (t - 1):128 * t] = v
                u_ref[8 * g:8 * g + 8, 128 * t:128 * t + 128] = v
        return carry

    r_ref[...] = e_ref[0:16, :]
    u_ref[...] = jnp.zeros_like(u_ref)
    if unroll:
        for k in range(8):
            body(k, 0)
    else:
        lax.fori_loop(0, 8, body, 0)


def chol_inverse(a_ref, w_ref, e1, r1, u1, y1, e2, r2, u2, y2, unroll=False):
    eye = (lax.broadcasted_iota(jnp.int32, (H, H), 0) == lax.broadcasted_iota(jnp.int32, (H, H), 1)).astype(F32)
    e1[0:H, 0:2 * H] = a_ref[0:H, :]
    e1[0:H, 2 * H:3 * H] = eye
    e1[H:, :] = jnp.zeros_like(e1[H:, :])
    stage(e1, r1, u1, y1, 2, unroll)
    u12 = y1[:, 0:H]
    e2[0:H, 0:H] = a_ref[H:2 * H, H:2 * H] - dot_tn(u12, u12)
    e2[0:H, H:2 * H] = eye
    e2[H:, :] = jnp.zeros_like(e2[H:, :])
    v = dot_tn(u12, y1[:, H:2 * H])
    stage(e2, r2, u2, y2, 1, unroll)
    w_ref[0:H, 0:H] = y1[:, H:2 * H]
    w_ref[0:H, H:2 * H] = jnp.zeros((H, H), F32)
    w_ref[H:2 * H, 0:H] = -dot_nn(y2[...], v)
    w_ref[H:2 * H, H:2 * H] = y2[...]


SCRATCH = [pltpu.VMEM((144, 384), F32), pltpu.VMEM((16, 384), F32), pltpu.VMEM((16, 384), F32), pltpu.VMEM((128, 256), F32),
           pltpu.VMEM((144, 256), F32), pltpu.VMEM((16, 256), F32), pltpu.VMEM((16, 256), F32), pltpu.VMEM((128, 128), F32)]


MESH = pl.DeviceIdType.MESH
BF16 = jnp.bfloat16


def remote(src, dst, send, recv, to):
    return pltpu.make_async_remote_copy(
        src_ref=src, dst_ref=dst, send_sem=send, recv_sem=recv, device_id=to, device_id_type=MESH
    )


def each_along_z(act):
    act(8)

    def pair(k, carry):
        act(8 - k)
        act(8 + k)
        return carry

    lax.fori_loop(1, 8, pair, 0)


def gather_and_factor(
    own_ref, pa_ref, pb_ref, q_ref, w_ref,
    d_ref, a_ref, e1, r1, u1, y1, e2, r2, u2, y2,
    d1_send, d1_recv, dy_send, dy_recv, q1_send, q1_recv, q2_send, q2_recv, q3_send, q3_recv, w_send, w_recv,
    xa_send, xa_recv, yb_send, yb_recv, ya_send, ya_recv, xb_send, xb_recv, own_sem,
):
    prow, pcol = lax.axis_index("prow"), lax.axis_index("pcol")
    z, core = prow // 2, prow % 2
    y, x = pcol // 4, pcol % 4
    peer = (z * 2 + 1 - core, pcol)
    source = jnp.logical_and(prow < 16, pcol < 2)
    self_lead = jnp.logical_and(prow == 1, pcol == 1)
    mine = z % 4 == y
    factors, leads = core == 0, core == 1

    def along_z(d):
        return (lax.rem(z + d, 16) * 2 + core, pcol)

    def along_x(d):
        return (prow, y * 4 + lax.rem(x + d, 4))

    def along_y(d):
        return (prow, lax.rem(y + d, 4) * 4 + x)

    barrier = pltpu.get_barrier_semaphore()

    def greet(to):
        pl.semaphore_signal(barrier, inc=1, device_id=to, device_id_type=MESH)

    @pl.when(leads)
    def _():
        each_along_z(lambda d: greet(along_z(d)))
        greet((pcol, 0))

        @pl.when(jnp.logical_not(self_lead))
        def _():
            greet((pcol, 1))

    @pl.when(factors)
    def _():
        for a in range(4):
            @pl.when(4 * a + y != z)
            def _():
                greet(((4 * a + y) * 2, pcol))
                greet(((4 * a + y) * 2 + 1, pcol))

    for d in (1, 2, 3):
        greet(along_x(d))
        greet(along_y(d))
    greet(peer)

    top, low, diag = own_ref.at[pl.ds(0, 64), :], own_ref.at[pl.ds(64, 64), :], own_ref.at[pl.ds(128, 8), :]
    own = [
        pltpu.make_async_copy(top, pa_ref.at[y, x], own_sem.at[0]),
        pltpu.make_async_copy(low, pb_ref.at[y, x], own_sem.at[1]),
    ]
    own_diag = pltpu.make_async_copy(diag, d_ref.at[z % 4, z // 4, 0], own_sem.at[2])
    own_lead = pltpu.make_async_copy(own_ref.at[pl.ds(0, 8), :], q_ref.at[1, z], own_sem.at[3])
    for copy in own:
        copy.start()

    @pl.when(jnp.logical_and(mine, factors))
    def _():
        own_diag.start()

    @pl.when(self_lead)
    def _():
        own_lead.start()

    others = jnp.where(mine, 15, 0) + jnp.where(leads, 15, 0) + jnp.where(source, 16, 0) - jnp.where(self_lead, 1, 0)
    pl.semaphore_wait(barrier, 7 + others)

    def q1(d):
        t = lax.rem(z + d, 16)
        rows = own_ref.at[pl.ds(pl.multiple_of(t * 8, 8), 8), :]
        return remote(rows, q_ref.at[pcol, t], q1_send.at[d], q1_recv.at[pcol], (t * 2 + 1, prow))

    def each_lead(act):
        @pl.when(source)
        def _():
            each_along_z(lambda d: act(q1(d)))

            @pl.when(jnp.logical_not(self_lead))
            def _():
                act(q1(0))

    each_lead(lambda copy: copy.start())

    def d1(d):
        to = (lax.rem(z + d, 16) * 2, pcol)
        return remote(diag, d_ref.at[z % 4, z // 4, core], d1_send.at[d], d1_recv.at[2 * d + core], to)

    def each_d1(act):
        @pl.when(mine)
        def _():
            each_along_z(lambda d: act(d1(d)))

            @pl.when(leads)
            def _():
                act(d1(0))

    each_d1(lambda copy: copy.start())

    def xa(d):
        return remote(top, pa_ref.at[y, x], xa_send.at[d], xa_recv.at[d], along_x(d))

    def yb(d):
        return remote(low, pb_ref.at[y, x], yb_send.at[d], yb_recv.at[d], along_y(d))

    for d in (2, 1, 3):
        xa(d).start()
        yb(d).start()

    def ya(d):
        return remote(pa_ref.at[y], pa_ref.at[y], ya_send.at[d], ya_recv.at[d], along_y(d))

    def xb(d):
        return remote(pb_ref.at[:, x], pb_ref.at[:, x], xb_send.at[d], xb_recv.at[d], along_x(d))

    def second_step():
        for copy in own:
            copy.wait()
        for d in (1, 3, 2):
            xa(d).wait_recv()
            yb(d).wait_recv()
        for d in (2, 1, 3):
            ya(d).start()
            xb(d).start()

    def dy(d):
        return remote(d_ref.at[y], d_ref.at[y], dy_send.at[d], dy_recv.at[d], along_y(d))

    def q2(d):
        return remote(q_ref.at[:, z], q_ref.at[:, z], q2_send.at[d], q2_recv.at[d], along_z(d))

    w_copy = remote(w_ref, w_ref, w_send.at[0], w_recv.at[0], peer)
    q_copy = remote(q_ref, q_ref, q3_send.at[0], q3_recv.at[0], peer)

    @pl.when(factors)
    def _():
        for a in range(4):
            away = lax.rem(z - (4 * a + y) + 16, 16)
            for k in range(2):
                def arrived():
                    remote(diag, d_ref.at[y, a, k], d1_send.at[0], d1_recv.at[2 * away + k], peer).wait_recv()

                if k == 0:
                    pl.when(away != 0)(arrived)
                else:
                    arrived()

        @pl.when(mine)
        def _():
            own_diag.wait()

        for d in (2, 1, 3):
            dy(d).start()
        for d in (1, 3, 2):
            dy(d).wait_recv()
        second_step()
        for t in range(16):
            for c in range(2):
                a_ref[t * 16 + c * 8:t * 16 + c * 8 + 8, :] = d_ref[t % 4, t // 4, c]
        chol_inverse(a_ref, w_ref, e1, r1, u1, y1, e2, r2, u2, y2)
        w_copy.start()
        for d in (1, 3, 2):
            dy(d).wait_send()
        w_copy.wait_send()
        q_copy.wait_recv()

    @pl.when(leads)
    def _():
        second_step()
        remote(q_ref.at[0, z], q_ref.at[0, z], q1_send.at[0], q1_recv.at[0], peer).wait_recv()

        @pl.when(jnp.logical_not(self_lead))
        def _():
            remote(q_ref.at[1, z], q_ref.at[1, z], q1_send.at[0], q1_recv.at[1], peer).wait_recv()

        @pl.when(self_lead)
        def _():
            own_lead.wait()

        each_along_z(lambda d: q2(d).start())
        each_along_z(lambda d: q2(d).wait_recv())
        q_copy.start()
        each_along_z(lambda d: q2(d).wait_send())
        w_copy.wait_recv()
        q_copy.wait_send()

    for d in (1, 3, 2):
        ya(d).wait_recv()
        xb(d).wait_recv()
        xa(d).wait_send()
        yb(d).wait_send()
        ya(d).wait_send()
        xb(d).wait_send()
    each_d1(lambda copy: copy.wait_send())
    each_lead(lambda copy: copy.wait_send())


def halves(v):
    high = v.astype(BF16)
    return high, (v - high.astype(F32)).astype(BF16)


def dot3(a, b):
    def one(p, q):
        return lax.dot_general(p, q, (((1,), (1,)), ((), ())), preferred_element_type=F32)

    return one(a[0], b[0]) + (one(a[0], b[1]) + one(a[1], b[0]))


def update(pa_ref, pb_ref, t_ref, w_ref, q_ref, own_ref, u_ref, s_ref, u_buf, s_buf, u_sem, s_sem):
    w = halves(w_ref[...])
    s_buf[...] = dot3(halves(own_ref[0:128, :]), w)
    s_copy = pltpu.make_async_copy(s_buf, s_ref, s_sem.at[0])
    s_copy.start()
    q = halves(dot3(halves(q_ref[...]), w))
    copies = []
    for i in range(8):
        rows = jnp.concatenate([pa_ref[2 * i], pb_ref[2 * i], pa_ref[2 * i + 1], pb_ref[2 * i + 1]], axis=0)
        solved = dot3(halves(rows), w)
        part = pl.ds(256 * i, 256)
        u_buf[part, :] = t_ref[part, :] - dot3(halves(solved), q)
        copy = pltpu.make_async_copy(u_buf.at[part, :], u_ref.at[part, :], u_sem.at[i])
        copy.start()
        copies.append(copy)
    for copy in copies:
        copy.wait()
    s_copy.wait()


def per_device(diag_block, panel, trailing):
    rows, more = panel.shape[0], diag_block.shape[0]
    low_panel = lax.pad(panel, jnp.float32(0), ((0, more, 0), (0, 0, 0)))
    high_diag = lax.pad(diag_block, jnp.float32(0), ((rows, 0, 0), (0, 0, 0)))
    own = jnp.where(lax.broadcasted_iota(jnp.int32, low_panel.shape, 0) < rows, low_panel, high_diag)
    hbm = pl.BlockSpec(memory_space=pltpu.HBM)
    vmem = pl.BlockSpec(memory_space=pltpu.VMEM)
    dma = pltpu.SemaphoreType.DMA
    pa, pb, q, w = pl.pallas_call(
        gather_and_factor,
        out_shape=(
            jax.ShapeDtypeStruct((4, 4, 64, 256), F32),
            jax.ShapeDtypeStruct((4, 4, 64, 256), F32),
            jax.ShapeDtypeStruct((2, 16, 8, 256), F32),
            jax.ShapeDtypeStruct((256, 256), F32),
        ),
        in_specs=[vmem],
        out_specs=(vmem,) * 4,
        scratch_shapes=[pltpu.VMEM((4, 4, 2, 8, 256), F32), pltpu.VMEM((256, 256), F32)] + SCRATCH + [
            dma((16,)), dma((32,)), dma((4,)), dma((4,)), dma((16,)), dma((2,)), dma((16,)), dma((16,)), dma((1,)), dma((1,)), dma((1,)), dma((1,)),
            dma((4,)), dma((4,)), dma((4,)), dma((4,)), dma((4,)), dma((4,)), dma((4,)), dma((4,)), dma((4,)),
        ],
        cost_estimate=pl.CostEstimate(flops=10**10, bytes_accessed=80 * 10**6, transcendentals=0),
        compiler_params=pltpu.CompilerParams(collective_id=0, has_side_effects=True, vmem_limit_bytes=32 << 20),
    )(own)
    pa, pb, q = pa.reshape(16, 64, 256), pb.reshape(16, 64, 256), q.reshape(256, 256)
    return pl.pallas_call(
        update,
        out_shape=(jax.ShapeDtypeStruct((2048, 256), F32), jax.ShapeDtypeStruct((128, 256), F32)),
        in_specs=[vmem] * 6,
        out_specs=(hbm, hbm),
        scratch_shapes=[pltpu.VMEM((2048, 256), F32), pltpu.VMEM((128, 256), F32), dma((8,)), dma((1,))],
        compiler_params=pltpu.CompilerParams(vmem_limit_bytes=32 << 20),
    )(pa, pb, trailing, w, q, own)


def solution(mesh):
    in_specs = (P("prow", None), P(("prow", "pcol"), None), P("prow", "pcol"))
    out_specs = (P("prow", "pcol"), P(("prow", "pcol"), None))
    return jax.shard_map(
        per_device, mesh=mesh, in_specs=in_specs, out_specs=out_specs, check_vma=False
    )
```

```python
import functools

import jax
import jax.numpy as jnp
from jax import lax
from jax.experimental import pallas as pl
from jax.experimental.pallas import tpu as pltpu
from jax.sharding import PartitionSpec as P

HI = lax.Precision.HIGHEST
F32 = jnp.float32
NBK = 16
H = 128

def sub(x, s):
    return jnp.broadcast_to(x[s:s + 1, :], (8, 128))

def lane(x, c):
    return jnp.broadcast_to(x[:, c:c + 1], (8, 128))

def dot_tn(a, b):
    return lax.dot_general(a, b, (((0,), (0,)), ((), ())), precision=HI, preferred_element_type=F32)

def dot_nn(a, b):
    return lax.dot_general(a, b, (((1,), (0,)), ((), ())), precision=HI, preferred_element_type=F32)

def update_tn(u):
    rest = u
    parts = []
    for _ in range(3):
        parts.append(rest.astype(jnp.bfloat16))
        rest = rest - parts[-1].astype(F32)
    h, m, l = parts
    left = jnp.concatenate([p[:, 0:H] for p in (h, h, h, m, m, l)], axis=0)
    right = jnp.concatenate([h, m, l, h, m, h], axis=0)
    return lax.dot_general(left, right, (((0,), (0,)), ((), ())), preferred_element_type=F32)


def stage(e_ref, r_ref, u_ref, y_ref, tiles):
    iota = lax.broadcasted_iota(jnp.int32, (8, 128), 0)

    def body(k, carry):
        e_ref[0:H, :] = e_ref[0:H, :] - update_tn(u_ref[...])

        r = [[r_ref[8 * g:8 * g + 8, 128 * t:128 * t + 128] for t in range(tiles + 1)] for g in range(2)]
        b = [[lane(r[g][0], j) if (g == 1 or j < 8) else None for g in range(2)] for j in range(16)]
        rot = [pltpu.roll(r[g][0], H - NBK, 1) for g in range(2)]
        nxt = jnp.concatenate(rot, axis=0).T[0:16, :]
        gm = [[lane(nxt[8 * g:8 * g + 8, :], j) for g in range(2)] for j in range(16)]
        for g in range(2):
            r[g][0] = rot[g]
        scale = [None, None]
        rows = []
        gs = []
        for j in range(16):
            gj, sj = divmod(j, 8)
            if j == 0:
                p = sub(b[0][0], 0)
            f = 1.0 / p
            rs = lax.rsqrt(p)
            m = [None, None]
            for g in range(gj, 2):
                m[g] = b[j][g] * f
            scale[gj] = rs if sj == 0 else jnp.where(iota >= sj, rs, scale[gj])
            if j < 15:
                gn, sn = divmod(j + 1, 8)
                across = sub(b[j][gn], sn)
                p = sub(b[j + 1][gn], sn) - (across * f) * across
            g0 = gm[j][0] * f
            g1 = gm[j][1] * f
            gs.append((g0, g1))
            for c in range(j + 1, 16):
                gc, sc = divmod(c, 8)
                a = sub(b[j][gc], sc)
                for g in range(gc, 2):
                    b[c][g] = b[c][g] - m[g] * a
                gm[c][0] = gm[c][0] - g0 * a
                gm[c][1] = gm[c][1] - g1 * a
            row = [sub(r[gj][t], sj) for t in range(tiles + 1)]
            rows.append(row)
            for g in range(gj, 2):
                mm = jnp.where(iota > sj, m[g], 0.0) if g == gj else m[g]
                if g == gj and sj == 7:
                    continue
                for t in range(tiles + 1):
                    r[g][t] = r[g][t] - mm * row[t]
        base = pl.multiple_of((k + 1) * NBK, NBK)
        for g in range(2):
            for t in range(tiles + 1):
                acc = e_ref[pl.ds(base + 8 * g, 8), 128 * t:128 * t + 128]
                if t == 0:
                    acc = pltpu.roll(acc, lax.rem(2 * H - NBK * (k + 1), H), 1)
                for j in range(16):
                    acc = acc - gs[j][g] * rows[j][t]
                r_ref[8 * g:8 * g + 8, 128 * t:128 * t + 128] = acc
        here = pl.multiple_of(k * NBK, NBK)
        for g in range(2):
            for t in range(tiles + 1):
                v = r[g][t] * scale[g]
                if t == 0:
                    v = pltpu.roll(v, lax.rem(NBK * (k + 1), H), 1)
                else:
                    y_ref[pl.ds(here + 8 * g, 8), 128 * (t - 1):128 * t] = v
                u_ref[8 * g:8 * g + 8, 128 * t:128 * t + 128] = v
        return carry

    r_ref[...] = e_ref[0:16, :]
    lax.fori_loop(0, 8, body, 0)


def prepare(e1, u1, e2, u2):
    eye = (lax.broadcasted_iota(jnp.int32, (H, H), 0) == lax.broadcasted_iota(jnp.int32, (H, H), 1)).astype(F32)
    e1[0:H, 2 * H:3 * H] = eye
    e1[H:, :] = jnp.zeros_like(e1[H:, :])
    u1[...] = jnp.zeros_like(u1)
    e2[0:H, H:2 * H] = eye
    e2[H:, :] = jnp.zeros_like(e2[H:, :])
    u2[...] = jnp.zeros_like(u2)


def chol_inverse(w_ref, e1, r1, u1, y1, e2, r2, u2, y2):
    stage(e1, r1, u1, y1, 2)
    u12 = y1[:, 0:H]
    e2[0:H, 0:H] = e2[0:H, 0:H] - dot_tn(u12, u12)
    v = dot_tn(u12, y1[:, H:2 * H])
    stage(e2, r2, u2, y2, 1)
    w_ref[0:H, 0:H] = y1[:, H:2 * H]
    w_ref[0:H, H:2 * H] = jnp.zeros((H, H), F32)
    w_ref[H:2 * H, 0:H] = -dot_nn(y2[...], v)
    w_ref[H:2 * H, H:2 * H] = y2[...]


SCRATCH = [pltpu.VMEM((144, 384), F32), pltpu.VMEM((16, 384), F32), pltpu.VMEM((16, 384), F32), pltpu.VMEM((128, 256), F32),
           pltpu.VMEM((144, 256), F32), pltpu.VMEM((16, 256), F32), pltpu.VMEM((16, 256), F32), pltpu.VMEM((128, 128), F32)]


MESH = pl.DeviceIdType.MESH
BF16 = jnp.bfloat16


def remote(src, dst, send, recv, to):
    return pltpu.make_async_remote_copy(
        src_ref=src, dst_ref=dst, send_sem=send, recv_sem=recv, device_id=to, device_id_type=MESH
    )


def part(rows, right):
    return rows.at[..., pl.ds(H, H)] if right else rows


def each_along_z(act):
    act(8)

    def pair(k, carry):
        act(8 - k)
        act(8 + k)
        return carry

    lax.fori_loop(1, 8, pair, 0)


def gather_and_factor(
    own_ref, pa_ref, pb_ref, q_ref, w_ref,
    d_ref, e1, r1, u1, y1, e2, r2, u2, y2,
    d1_send, d1_recv, dy_send, dy_recv, q1_send, q1_recv, q2_send, q2_recv, q3_send, q3_recv, w_send, w_recv,
    xa_send, xa_recv, yb_send, yb_recv, ya_send, ya_recv, xb_send, xb_recv, own_sem,
):
    prow, pcol = lax.axis_index("prow"), lax.axis_index("pcol")
    z, core = prow // 2, prow % 2
    y, x = pcol // 4, pcol % 4
    peer = (z * 2 + 1 - core, pcol)
    source = jnp.logical_and(prow < 16, pcol < 2)
    self_lead = jnp.logical_and(prow == 1, pcol == 1)
    mine = z % 4 == y
    factors, leads = core == 0, core == 1

    def along_z(d):
        return (lax.rem(z + d, 16) * 2 + core, pcol)

    def along_x(d):
        return (prow, y * 4 + lax.rem(x + d, 4))

    def along_y(d):
        return (prow, lax.rem(y + d, 4) * 4 + x)

    barrier = pltpu.get_barrier_semaphore()

    def greet(to):
        pl.semaphore_signal(barrier, inc=1, device_id=to, device_id_type=MESH)

    @pl.when(leads)
    def _():
        each_along_z(lambda d: greet(along_z(d)))
        greet((pcol, 0))

        @pl.when(jnp.logical_not(self_lead))
        def _():
            greet((pcol, 1))

    @pl.when(factors)
    def _():
        for a in range(4):
            @pl.when(4 * a + y != z)
            def _():
                greet(((4 * a + y) * 2, pcol))
                greet(((4 * a + y) * 2 + 1, pcol))

    for d in (1, 2, 3):
        greet(along_x(d))
        greet(along_y(d))
    greet(peer)

    top, low, diag = own_ref.at[pl.ds(0, 64), :], own_ref.at[pl.ds(64, 64), :], own_ref.at[pl.ds(128, 8), :]
    own = [
        pltpu.make_async_copy(top, pa_ref.at[y, x], own_sem.at[0]),
        pltpu.make_async_copy(low, pb_ref.at[y, x], own_sem.at[1]),
    ]
    own_diag = pltpu.make_async_copy(diag, d_ref.at[z % 4, z // 4, 0], own_sem.at[2])
    own_lead = pltpu.make_async_copy(own_ref.at[pl.ds(0, 8), :], q_ref.at[1, z], own_sem.at[3])
    for copy in own:
        copy.start()

    @pl.when(jnp.logical_and(mine, factors))
    def _():
        own_diag.start()

    @pl.when(self_lead)
    def _():
        own_lead.start()

    @pl.when(factors)
    def _():
        prepare(e1, u1, e2, u2)

    others = jnp.where(mine, 15, 0) + jnp.where(leads, 15, 0) + jnp.where(source, 16, 0) - jnp.where(self_lead, 1, 0)
    pl.semaphore_wait(barrier, 7 + others)

    def q1(d):
        t = lax.rem(z + d, 16)
        rows = own_ref.at[pl.ds(pl.multiple_of(t * 8, 8), 8), :]
        return remote(rows, q_ref.at[pcol, t], q1_send.at[d], q1_recv.at[pcol], (t * 2 + 1, prow))

    def each_lead(act):
        @pl.when(source)
        def _():
            each_along_z(lambda d: act(q1(d)))

            @pl.when(jnp.logical_not(self_lead))
            def _():
                act(q1(0))

    each_lead(lambda copy: copy.start())

    def d1(d, right):
        to = (lax.rem(z + d, 16) * 2, pcol)
        return remote(part(diag, right), part(d_ref.at[z % 4, z // 4, core], right), d1_send.at[d], d1_recv.at[2 * d + core], to)

    def each_d1(act):
        for right in (False, True):
            @pl.when(jnp.logical_and(mine, (z >= 8) == right))
            def _():
                each_along_z(lambda d: act(d1(d, right)))

                @pl.when(leads)
                def _():
                    act(d1(0, right))

    each_d1(lambda copy: copy.start())

    def xa(d):
        return remote(top, pa_ref.at[y, x], xa_send.at[d], xa_recv.at[d], along_x(d))

    def yb(d):
        return remote(low, pb_ref.at[y, x], yb_send.at[d], yb_recv.at[d], along_y(d))

    for d in (2, 1, 3):
        xa(d).start()
        yb(d).start()

    def ya(d):
        return remote(pa_ref.at[y], pa_ref.at[y], ya_send.at[d], ya_recv.at[d], along_y(d))

    def xb(d):
        return remote(pb_ref.at[:, x], pb_ref.at[:, x], xb_send.at[d], xb_recv.at[d], along_x(d))

    def second_step():
        for copy in own:
            copy.wait()
        for d in (1, 3, 2):
            xa(d).wait_recv()
            yb(d).wait_recv()
        for d in (2, 1, 3):
            ya(d).start()
            xb(d).start()

    def dy(d, right):
        rows = part(d_ref.at[y, pl.ds(2, 2)], True) if right else d_ref.at[y, pl.ds(0, 2)]
        k = 4 * int(right) + d
        return remote(rows, rows, dy_send.at[k], dy_recv.at[k], along_y(d))

    def q2(d):
        return remote(q_ref.at[:, z], q_ref.at[:, z], q2_send.at[d], q2_recv.at[d], along_z(d))

    w_copy = remote(w_ref, w_ref, w_send.at[0], w_recv.at[0], peer)
    q_copy = remote(q_ref, q_ref, q3_send.at[0], q3_recv.at[0], peer)

    @pl.when(factors)
    def _():
        for a in range(4):
            away = lax.rem(z - (4 * a + y) + 16, 16)
            for k in range(2):
                def arrived():
                    rows = part(d_ref.at[y, a, k], a >= 2)
                    remote(rows, rows, d1_send.at[0], d1_recv.at[2 * away + k], peer).wait_recv()

                if k == 0:
                    pl.when(away != 0)(arrived)
                else:
                    arrived()

        @pl.when(mine)
        def _():
            own_diag.wait()

        for right in (False, True):
            for d in (2, 1, 3):
                dy(d, right).start()
        for right in (False, True):
            for d in (1, 3, 2):
                dy(d, right).wait_recv()
        second_step()
        for t in range(8):
            for k in range(2):
                at = t * 16 + k * 8
                e1[at:at + 8, 0:2 * H] = d_ref[t % 4, t // 4, k]
                e2[at:at + 8, 0:H] = d_ref[t % 4, 2 + t // 4, k, :, H:2 * H]
        chol_inverse(w_ref, e1, r1, u1, y1, e2, r2, u2, y2)
        w_copy.start()
        for right in (False, True):
            for d in (1, 3, 2):
                dy(d, right).wait_send()
        w_copy.wait_send()
        q_copy.wait_recv()

    @pl.when(leads)
    def _():
        second_step()
        remote(q_ref.at[0, z], q_ref.at[0, z], q1_send.at[0], q1_recv.at[0], peer).wait_recv()

        @pl.when(jnp.logical_not(self_lead))
        def _():
            remote(q_ref.at[1, z], q_ref.at[1, z], q1_send.at[0], q1_recv.at[1], peer).wait_recv()

        @pl.when(self_lead)
        def _():
            own_lead.wait()

        each_along_z(lambda d: q2(d).start())
        each_along_z(lambda d: q2(d).wait_recv())
        q_copy.start()
        each_along_z(lambda d: q2(d).wait_send())
        w_copy.wait_recv()
        q_copy.wait_send()

    for d in (1, 3, 2):
        ya(d).wait_recv()
        xb(d).wait_recv()
        xa(d).wait_send()
        yb(d).wait_send()
        ya(d).wait_send()
        xb(d).wait_send()
    each_d1(lambda copy: copy.wait_send())
    each_lead(lambda copy: copy.wait_send())


def halves(v):
    high = v.astype(BF16)
    return high, (v - high.astype(F32)).astype(BF16)


def dot3(a, b):
    def one(p, q):
        return lax.dot_general(p, q, (((1,), (1,)), ((), ())), preferred_element_type=F32)

    return one(a[0], b[0]) + (one(a[0], b[1]) + one(a[1], b[0]))


def update(pa_ref, pb_ref, t_ref, w_ref, q_ref, own_ref, u_ref, s_ref, u_buf, s_buf, u_sem, s_sem):
    w = halves(w_ref[...])
    s_buf[...] = dot3(halves(own_ref[0:128, :]), w)
    s_copy = pltpu.make_async_copy(s_buf, s_ref, s_sem.at[0])
    s_copy.start()
    q = halves(dot3(halves(q_ref[...]), w))
    copies = []
    for i in range(8):
        rows = jnp.concatenate([pa_ref[2 * i], pb_ref[2 * i], pa_ref[2 * i + 1], pb_ref[2 * i + 1]], axis=0)
        solved = dot3(halves(rows), w)
        part = pl.ds(256 * i, 256)
        u_buf[part, :] = t_ref[part, :] - dot3(halves(solved), q)
        copy = pltpu.make_async_copy(u_buf.at[part, :], u_ref.at[part, :], u_sem.at[i])
        copy.start()
        copies.append(copy)
    for copy in copies:
        copy.wait()
    s_copy.wait()


def per_device(diag_block, panel, trailing):
    rows, more = panel.shape[0], diag_block.shape[0]
    low_panel = lax.pad(panel, jnp.float32(0), ((0, more, 0), (0, 0, 0)))
    high_diag = lax.pad(diag_block, jnp.float32(0), ((rows, 0, 0), (0, 0, 0)))
    own = jnp.where(lax.broadcasted_iota(jnp.int32, low_panel.shape, 0) < rows, low_panel, high_diag)
    hbm = pl.BlockSpec(memory_space=pltpu.HBM)
    vmem = pl.BlockSpec(memory_space=pltpu.VMEM)
    dma = pltpu.SemaphoreType.DMA
    pa, pb, q, w = pl.pallas_call(
        gather_and_factor,
        out_shape=(
            jax.ShapeDtypeStruct((4, 4, 64, 256), F32),
            jax.ShapeDtypeStruct((4, 4, 64, 256), F32),
            jax.ShapeDtypeStruct((2, 16, 8, 256), F32),
            jax.ShapeDtypeStruct((256, 256), F32),
        ),
        in_specs=[vmem],
        out_specs=(vmem,) * 4,
        scratch_shapes=[pltpu.VMEM((4, 4, 2, 8, 256), F32)] + SCRATCH + [
            dma((16,)), dma((32,)), dma((8,)), dma((8,)), dma((16,)), dma((2,)), dma((16,)), dma((16,)), dma((1,)), dma((1,)), dma((1,)), dma((1,)),
            dma((4,)), dma((4,)), dma((4,)), dma((4,)), dma((4,)), dma((4,)), dma((4,)), dma((4,)), dma((4,)),
        ],
        cost_estimate=pl.CostEstimate(flops=10**10, bytes_accessed=80 * 10**6, transcendentals=0),
        compiler_params=pltpu.CompilerParams(collective_id=0, has_side_effects=True, vmem_limit_bytes=32 << 20),
    )(own)
    pa, pb, q = pa.reshape(16, 64, 256), pb.reshape(16, 64, 256), q.reshape(256, 256)
    return pl.pallas_call(
        update,
        out_shape=(jax.ShapeDtypeStruct((2048, 256), F32), jax.ShapeDtypeStruct((128, 256), F32)),
        in_specs=[vmem] * 6,
        out_specs=(hbm, hbm),
        scratch_shapes=[pltpu.VMEM((2048, 256), F32), pltpu.VMEM((128, 256), F32), dma((8,)), dma((1,))],
        compiler_params=pltpu.CompilerParams(vmem_limit_bytes=32 << 20),
    )(pa, pb, trailing, w, q, own)


def solution(mesh):
    in_specs = (P("prow", None), P(("prow", "pcol"), None), P("prow", "pcol"))
    out_specs = (P("prow", "pcol"), P(("prow", "pcol"), None))
    return jax.shard_map(
        per_device, mesh=mesh, in_specs=in_specs, out_specs=out_specs, check_vma=False
    )
```

```python
import functools

import jax
import jax.numpy as jnp
from jax import lax
from jax.experimental import pallas as pl
from jax.experimental.pallas import tpu as pltpu
from jax.sharding import PartitionSpec as P

HI = lax.Precision.HIGHEST
F32 = jnp.float32
NBK = 16
H = 128

def sub(x, s):
    return jnp.broadcast_to(x[s:s + 1, :], (8, 128))

def lane(x, c):
    return jnp.broadcast_to(x[:, c:c + 1], (8, 128))

def dot_tn(a, b):
    return lax.dot_general(a, b, (((0,), (0,)), ((), ())), precision=HI, preferred_element_type=F32)

def dot_nn(a, b):
    return lax.dot_general(a, b, (((1,), (0,)), ((), ())), precision=HI, preferred_element_type=F32)

def update_tn(u):
    rest = u
    parts = []
    for _ in range(3):
        parts.append(rest.astype(jnp.bfloat16))
        rest = rest - parts[-1].astype(F32)
    h, m, l = parts
    left = jnp.concatenate([p[:, 0:H] for p in (h, h, h, m, m, l)], axis=0)
    right = jnp.concatenate([h, m, l, h, m, h], axis=0)
    return lax.dot_general(left, right, (((0,), (0,)), ((), ())), preferred_element_type=F32)


def stage(e_ref, r_ref, u_ref, y_ref, tiles):
    iota = lax.broadcasted_iota(jnp.int32, (8, 128), 0)

    def body(k, carry):
        e_ref[0:H, :] = e_ref[0:H, :] - update_tn(u_ref[...])

        r = [[r_ref[8 * g:8 * g + 8, 128 * t:128 * t + 128] for t in range(tiles + 1)] for g in range(2)]
        b = [[lane(r[g][0], j) if (g == 1 or j < 8) else None for g in range(2)] for j in range(16)]
        rot = [pltpu.roll(r[g][0], H - NBK, 1) for g in range(2)]
        nxt = jnp.concatenate(rot, axis=0).T[0:16, :]
        gm = [[lane(nxt[8 * g:8 * g + 8, :], j) for g in range(2)] for j in range(16)]
        for g in range(2):
            r[g][0] = rot[g]
        done = [[None] * (tiles + 1) for g in range(2)]
        rows = []
        gs = []
        p = sub(b[0][0], 0)
        for j in range(16):
            gj, sj = divmod(j, 8)
            f = lax.rsqrt(p)
            m = [None, None]
            for g in range(gj, 2):
                m[g] = b[j][g] * f
            if j < 15:
                gn, sn = divmod(j + 1, 8)
                across = sub(b[j][gn], sn) * f
                p = sub(b[j + 1][gn], sn) - across * across
            g0 = gm[j][0] * f
            g1 = gm[j][1] * f
            gs.append((g0, g1))
            for c in range(j + 1, 16):
                gc, sc = divmod(c, 8)
                a = sub(m[gc], sc)
                for g in range(gc, 2):
                    b[c][g] = b[c][g] - m[g] * a
                gm[c][0] = gm[c][0] - g0 * a
                gm[c][1] = gm[c][1] - g1 * a
            row = [sub(r[gj][t], sj) * f for t in range(tiles + 1)]
            rows.append(row)
            for t in range(tiles + 1):
                done[gj][t] = row[t] if sj == 0 else jnp.where(iota >= sj, row[t], done[gj][t])
            for g in range(gj, 2):
                if g == gj and sj == 7:
                    continue
                for t in range(tiles + 1):
                    r[g][t] = r[g][t] - m[g] * row[t]
        base = pl.multiple_of((k + 1) * NBK, NBK)
        for g in range(2):
            for t in range(tiles + 1):
                acc = e_ref[pl.ds(base + 8 * g, 8), 128 * t:128 * t + 128]
                if t == 0:
                    acc = pltpu.roll(acc, lax.rem(2 * H - NBK * (k + 1), H), 1)
                for j in range(16):
                    acc = acc - gs[j][g] * rows[j][t]
                r_ref[8 * g:8 * g + 8, 128 * t:128 * t + 128] = acc
        here = pl.multiple_of(k * NBK, NBK)
        for g in range(2):
            for t in range(tiles + 1):
                v = done[g][t]
                if t == 0:
                    v = pltpu.roll(v, lax.rem(NBK * (k + 1), H), 1)
                else:
                    y_ref[pl.ds(here + 8 * g, 8), 128 * (t - 1):128 * t] = v
                u_ref[8 * g:8 * g + 8, 128 * t:128 * t + 128] = v
        return carry

    r_ref[...] = e_ref[0:16, :]
    lax.fori_loop(0, 8, body, 0)


def prepare(e1, u1, e2, u2):
    eye = (lax.broadcasted_iota(jnp.int32, (H, H), 0) == lax.broadcasted_iota(jnp.int32, (H, H), 1)).astype(F32)
    e1[0:H, 2 * H:3 * H] = eye
    e1[H:, :] = jnp.zeros_like(e1[H:, :])
    u1[...] = jnp.zeros_like(u1)
    e2[0:H, H:2 * H] = eye
    e2[H:, :] = jnp.zeros_like(e2[H:, :])
    u2[...] = jnp.zeros_like(u2)


def chol_inverse(w_ref, upper_done, e1, r1, u1, y1, e2, r2, u2, y2):
    stage(e1, r1, u1, y1, 2)
    w_ref[0:H, 0:H] = y1[:, H:2 * H]
    w_ref[0:H, H:2 * H] = jnp.zeros((H, H), F32)
    upper_done()
    u12 = y1[:, 0:H]
    e2[0:H, 0:H] = e2[0:H, 0:H] - dot_tn(u12, u12)
    v = dot_tn(u12, y1[:, H:2 * H])
    stage(e2, r2, u2, y2, 1)
    w_ref[H:2 * H, 0:H] = -dot_nn(y2[...], v)
    w_ref[H:2 * H, H:2 * H] = y2[...]


SCRATCH = [pltpu.VMEM((144, 384), F32), pltpu.VMEM((16, 384), F32), pltpu.VMEM((16, 384), F32), pltpu.VMEM((128, 256), F32),
           pltpu.VMEM((144, 256), F32), pltpu.VMEM((16, 256), F32), pltpu.VMEM((16, 256), F32), pltpu.VMEM((128, 128), F32)]


MESH = pl.DeviceIdType.MESH
BF16 = jnp.bfloat16


def remote(src, dst, send, recv, to):
    return pltpu.make_async_remote_copy(
        src_ref=src, dst_ref=dst, send_sem=send, recv_sem=recv, device_id=to, device_id_type=MESH
    )


def part(rows, right):
    return rows.at[..., pl.ds(H, H)] if right else rows


def each_along_z(act):
    act(8)

    def pair(k, carry):
        act(8 - k)
        act(8 + k)
        return carry

    lax.fori_loop(1, 8, pair, 0)


def gather_and_factor(
    own_ref, pa_ref, pb_ref, q_ref, w_ref,
    d_ref, e1, r1, u1, y1, e2, r2, u2, y2,
    d1_send, d1_recv, dy_send, dy_recv, q1_send, q1_recv, q2_send, q2_recv, q3_send, q3_recv, w_send, w_recv,
    xa_send, xa_recv, yb_send, yb_recv, ya_send, ya_recv, xb_send, xb_recv, own_sem,
):
    prow, pcol = lax.axis_index("prow"), lax.axis_index("pcol")
    z, core = prow // 2, prow % 2
    y, x = pcol // 4, pcol % 4
    peer = (z * 2 + 1 - core, pcol)
    source = jnp.logical_and(prow < 16, pcol < 2)
    self_lead = jnp.logical_and(prow == 1, pcol == 1)
    mine = z % 4 == y
    factors, leads = core == 0, core == 1

    def along_z(d):
        return (lax.rem(z + d, 16) * 2 + core, pcol)

    def along_x(d):
        return (prow, y * 4 + lax.rem(x + d, 4))

    def along_y(d):
        return (prow, lax.rem(y + d, 4) * 4 + x)

    barrier = pltpu.get_barrier_semaphore()

    def greet(to):
        pl.semaphore_signal(barrier, inc=1, device_id=to, device_id_type=MESH)

    @pl.when(leads)
    def _():
        each_along_z(lambda d: greet(along_z(d)))
        greet((pcol, 0))

        @pl.when(jnp.logical_not(self_lead))
        def _():
            greet((pcol, 1))

    @pl.when(factors)
    def _():
        for a in range(4):
            @pl.when(4 * a + y != z)
            def _():
                greet(((4 * a + y) * 2, pcol))
                greet(((4 * a + y) * 2 + 1, pcol))

    for d in (1, 2, 3):
        greet(along_x(d))
        greet(along_y(d))
    greet(peer)

    top, low, diag = own_ref.at[pl.ds(0, 64), :], own_ref.at[pl.ds(64, 64), :], own_ref.at[pl.ds(128, 8), :]
    own = [
        pltpu.make_async_copy(top, pa_ref.at[y, x], own_sem.at[0]),
        pltpu.make_async_copy(low, pb_ref.at[y, x], own_sem.at[1]),
    ]
    own_diag = pltpu.make_async_copy(diag, d_ref.at[z % 4, z // 4, 0], own_sem.at[2])
    own_lead = pltpu.make_async_copy(own_ref.at[pl.ds(0, 8), :], q_ref.at[1, z], own_sem.at[3])
    for copy in own:
        copy.start()

    @pl.when(jnp.logical_and(mine, factors))
    def _():
        own_diag.start()

    @pl.when(self_lead)
    def _():
        own_lead.start()

    @pl.when(factors)
    def _():
        prepare(e1, u1, e2, u2)

    others = jnp.where(mine, 15, 0) + jnp.where(leads, 15, 0) + jnp.where(source, 16, 0) - jnp.where(self_lead, 1, 0)
    pl.semaphore_wait(barrier, 7 + others)

    def q1(d):
        t = lax.rem(z + d, 16)
        rows = own_ref.at[pl.ds(pl.multiple_of(t * 8, 8), 8), :]
        return remote(rows, q_ref.at[pcol, t], q1_send.at[d], q1_recv.at[pcol], (t * 2 + 1, prow))

    def each_lead(act):
        @pl.when(source)
        def _():
            each_along_z(lambda d: act(q1(d)))

            @pl.when(jnp.logical_not(self_lead))
            def _():
                act(q1(0))

    each_lead(lambda copy: copy.start())

    def d1(d, right):
        to = (lax.rem(z + d, 16) * 2, pcol)
        return remote(part(diag, right), part(d_ref.at[z % 4, z // 4, core], right), d1_send.at[d], d1_recv.at[2 * d + core], to)

    def each_d1(act):
        for right in (False, True):
            @pl.when(jnp.logical_and(mine, (z >= 8) == right))
            def _():
                each_along_z(lambda d: act(d1(d, right)))

                @pl.when(leads)
                def _():
                    act(d1(0, right))

    each_d1(lambda copy: copy.start())

    def xa(d):
        return remote(top, pa_ref.at[y, x], xa_send.at[d], xa_recv.at[d], along_x(d))

    def yb(d):
        return remote(low, pb_ref.at[y, x], yb_send.at[d], yb_recv.at[d], along_y(d))

    for d in (2, 1, 3):
        xa(d).start()
        yb(d).start()

    def ya(d):
        return remote(pa_ref.at[y], pa_ref.at[y], ya_send.at[d], ya_recv.at[d], along_y(d))

    def xb(d):
        return remote(pb_ref.at[:, x], pb_ref.at[:, x], xb_send.at[d], xb_recv.at[d], along_x(d))

    def second_step():
        for copy in own:
            copy.wait()
        for d in (1, 3, 2):
            xa(d).wait_recv()
            yb(d).wait_recv()
        for d in (2, 1, 3):
            ya(d).start()
            xb(d).start()

    def dy(d, right):
        rows = part(d_ref.at[y, pl.ds(2, 2)], True) if right else d_ref.at[y, pl.ds(0, 2)]
        k = 4 * int(right) + d
        return remote(rows, rows, dy_send.at[k], dy_recv.at[k], along_y(d))

    def q2(d):
        return remote(q_ref.at[:, z], q_ref.at[:, z], q2_send.at[d], q2_recv.at[d], along_z(d))

    def w_copy(i):
        rows = w_ref.at[pl.ds(128 * i, 128), :]
        return remote(rows, rows, w_send.at[i], w_recv.at[i], peer)

    q_copy = remote(q_ref, q_ref, q3_send.at[0], q3_recv.at[0], peer)

    def finish():
        for d in (1, 3, 2):
            ya(d).wait_recv()
            xb(d).wait_recv()
            xa(d).wait_send()
            yb(d).wait_send()
            ya(d).wait_send()
            xb(d).wait_send()
        each_d1(lambda copy: copy.wait_send())
        each_lead(lambda copy: copy.wait_send())

    @pl.when(factors)
    def _():
        for a in range(4):
            away = lax.rem(z - (4 * a + y) + 16, 16)
            for k in range(2):
                def arrived():
                    rows = part(d_ref.at[y, a, k], a >= 2)
                    remote(rows, rows, d1_send.at[0], d1_recv.at[2 * away + k], peer).wait_recv()

                if k == 0:
                    pl.when(away != 0)(arrived)
                else:
                    arrived()

        @pl.when(mine)
        def _():
            own_diag.wait()

        for right in (False, True):
            for d in (2, 1, 3):
                dy(d, right).start()
        second_step()
        for right in (False, True):
            for d in (1, 3, 2):
                dy(d, right).wait_recv()
        for t in range(8):
            for k in range(2):
                at = t * 16 + k * 8
                e1[at:at + 8, 0:2 * H] = d_ref[t % 4, t // 4, k]
                e2[at:at + 8, 0:H] = d_ref[t % 4, 2 + t // 4, k, :, H:2 * H]
        chol_inverse(w_ref, lambda: w_copy(0).start(), e1, r1, u1, y1, e2, r2, u2, y2)
        w_copy(1).start()
        for right in (False, True):
            for d in (1, 3, 2):
                dy(d, right).wait_send()
        finish()
        q_copy.wait_recv()
        for i in range(2):
            w_copy(i).wait_send()

    @pl.when(leads)
    def _():
        second_step()
        remote(q_ref.at[0, z], q_ref.at[0, z], q1_send.at[0], q1_recv.at[0], peer).wait_recv()

        @pl.when(jnp.logical_not(self_lead))
        def _():
            remote(q_ref.at[1, z], q_ref.at[1, z], q1_send.at[0], q1_recv.at[1], peer).wait_recv()

        @pl.when(self_lead)
        def _():
            own_lead.wait()

        each_along_z(lambda d: q2(d).start())
        each_along_z(lambda d: q2(d).wait_recv())
        q_copy.start()
        each_along_z(lambda d: q2(d).wait_send())
        finish()
        q_copy.wait_send()
        for i in range(2):
            w_copy(i).wait_recv()


def halves(v):
    high = v.astype(BF16)
    return high, (v - high.astype(F32)).astype(BF16)


def dot3(a, b):
    def one(p, q):
        return lax.dot_general(p, q, (((1,), (1,)), ((), ())), preferred_element_type=F32)

    return one(a[0], b[0]) + (one(a[0], b[1]) + one(a[1], b[0]))


def update(pa_ref, pb_ref, t_ref, w_ref, q_ref, own_ref, u_ref, s_ref, u_buf, s_buf, u_sem, s_sem):
    w = halves(w_ref[...])
    s_buf[...] = dot3(halves(own_ref[0:128, :]), w)
    s_copy = pltpu.make_async_copy(s_buf, s_ref, s_sem.at[0])
    s_copy.start()
    q = halves(dot3(halves(q_ref[...]), w))
    copies = []
    for i in range(8):
        rows = jnp.concatenate([pa_ref[2 * i], pb_ref[2 * i], pa_ref[2 * i + 1], pb_ref[2 * i + 1]], axis=0)
        solved = dot3(halves(rows), w)
        part = pl.ds(256 * i, 256)
        u_buf[part, :] = t_ref[part, :] - dot3(halves(solved), q)
        copy = pltpu.make_async_copy(u_buf.at[part, :], u_ref.at[part, :], u_sem.at[i])
        copy.start()
        copies.append(copy)
    for copy in copies:
        copy.wait()
    s_copy.wait()


def per_device(diag_block, panel, trailing):
    rows, more = panel.shape[0], diag_block.shape[0]
    low_panel = lax.pad(panel, jnp.float32(0), ((0, more, 0), (0, 0, 0)))
    high_diag = lax.pad(diag_block, jnp.float32(0), ((rows, 0, 0), (0, 0, 0)))
    own = jnp.where(lax.broadcasted_iota(jnp.int32, low_panel.shape, 0) < rows, low_panel, high_diag)
    hbm = pl.BlockSpec(memory_space=pltpu.HBM)
    vmem = pl.BlockSpec(memory_space=pltpu.VMEM)
    dma = pltpu.SemaphoreType.DMA
    pa, pb, q, w = pl.pallas_call(
        gather_and_factor,
        out_shape=(
            jax.ShapeDtypeStruct((4, 4, 64, 256), F32),
            jax.ShapeDtypeStruct((4, 4, 64, 256), F32),
            jax.ShapeDtypeStruct((2, 16, 8, 256), F32),
            jax.ShapeDtypeStruct((256, 256), F32),
        ),
        in_specs=[vmem],
        out_specs=(vmem,) * 4,
        scratch_shapes=[pltpu.VMEM((4, 4, 2, 8, 256), F32)] + SCRATCH + [
            dma((16,)), dma((32,)), dma((8,)), dma((8,)), dma((16,)), dma((2,)), dma((16,)), dma((16,)), dma((1,)), dma((1,)), dma((2,)), dma((2,)),
            dma((4,)), dma((4,)), dma((4,)), dma((4,)), dma((4,)), dma((4,)), dma((4,)), dma((4,)), dma((4,)),
        ],
        cost_estimate=pl.CostEstimate(flops=10**10, bytes_accessed=80 * 10**6, transcendentals=0),
        compiler_params=pltpu.CompilerParams(collective_id=0, has_side_effects=True, vmem_limit_bytes=32 << 20),
    )(own)
    pa, pb, q = pa.reshape(16, 64, 256), pb.reshape(16, 64, 256), q.reshape(256, 256)
    return pl.pallas_call(
        update,
        out_shape=(jax.ShapeDtypeStruct((2048, 256), F32), jax.ShapeDtypeStruct((128, 256), F32)),
        in_specs=[vmem] * 6,
        out_specs=(hbm, hbm),
        scratch_shapes=[pltpu.VMEM((2048, 256), F32), pltpu.VMEM((128, 256), F32), dma((8,)), dma((1,))],
        compiler_params=pltpu.CompilerParams(vmem_limit_bytes=32 << 20),
    )(pa, pb, trailing, w, q, own)


def solution(mesh):
    in_specs = (P("prow", None), P(("prow", "pcol"), None), P("prow", "pcol"))
    out_specs = (P("prow", "pcol"), P(("prow", "pcol"), None))
    return jax.shard_map(
        per_device, mesh=mesh, in_specs=in_specs, out_specs=out_specs, check_vma=False
    )
```
